256 devices in a mesh: tok: 32 (over x, z), head: 8 (over y, core).
Axes of the slice: x: 4, y: 4, z: 8, core: 2. Of those that a mesh axis runs over, the one named last changes fastest.
Arguments:
- queries: bfloat16 [32768, 4096], P(('tok', 'head')), may hold values from -6 to 6
- key_tokens: bfloat16 [32768, 4096], P(('tok', 'head')), may hold values from -6 to 6
- values: bfloat16 [32768, 4096], P(('tok', 'head')), may hold values from -6 to 6
- out_grad: bfloat16 [32768, 4096], P(('tok', 'head')), may hold values from -6 to 6
- learn_rates: float32 [32768, 16], P('tok', 'head'), may hold values from 0.2 to 2
- w_gate: bfloat16 [16, 256, 256], P('head'), may hold values from -0.375 to 0.375
- w_up: bfloat16 [16, 256, 256], P('head'), may hold values from -0.375 to 0.375
- w_down: bfloat16 [16, 256, 256], P('head'), may hold values from -0.375 to 0.375
Outputs:
- grad_queries: bfloat16 [32768, 4096], P(('tok', 'head'))
- grad_keys: bfloat16 [32768, 4096], P(('tok', 'head'))
- grad_values: bfloat16 [32768, 4096], P(('tok', 'head'))
The draws below stay inside these ranges and needn't reach their ends.
All inputs are finite; a program needn't handle non-finite values.
Results may differ from the reference program's by a relative error of at most 0.02.
Values may be sent and summed in bfloat16 or wider, within the bound.
A program may use at most 128 MiB of HBM per device.

```python
import math
import jax
import jax.numpy as jnp

H = 16
DH = 256
D = 4096
TOKENS = 32768


def shard_levels(key, extent, pieces, low, top_value):
    def one(position, shards_of):
        draws = jax.random.uniform(jax.random.fold_in(jax.random.fold_in(key, 6), position), (shards_of,), jnp.float32, low / len(pieces), top_value / len(pieces))
        return jnp.repeat(jnp.exp(draws), extent[position] // shards_of).reshape((-1,) + (1,) * (len(extent) - position - 1))

    level = one(*pieces[0])
    for cut in pieces[1:]:
        level = level * one(*cut)
    return level


def noise(key, shape, scale, reach, split=(), held_as=jnp.bfloat16):
    loudness = shard_levels(key, shape, split, -0.22, 0.18) if split else 1.0
    values = jax.random.normal(key, shape, jnp.float32) * scale * loudness
    return jnp.minimum(jnp.maximum(values, -reach), reach).astype(held_as)


def setup_inputs(seed: int = 0) -> dict:
    seeds = jax.random.split(jax.random.key(seed), 9)
    queries = noise(seeds[0], (TOKENS, D), 1.0, 6.0, ((0, 256),))
    key_tokens = noise(seeds[1], (TOKENS, D), 1.0, 6.0, ((0, 256),))
    values = noise(seeds[2], (TOKENS, D), 1.0, 6.0, ((0, 256),))
    out_grad = noise(seeds[3], (TOKENS, D), 1.0, 6.0, ((0, 256),))
    learn_rates = jnp.clip(jnp.exp(math.log(2.0) - 2.3025851 * jax.random.uniform(seeds[4], (TOKENS, H), jnp.float32) ** shard_levels(seeds[4], (TOKENS, H), ((0, 32), (1, 8)), -0.2, 0.2)), 0.2, 2.0)
    w_gate = noise(seeds[5], (H, DH, DH), DH ** -0.5, 0.375, ((0, 8),))
    w_up = noise(seeds[6], (H, DH, DH), DH ** -0.5, 0.375, ((0, 8),))
    w_down = noise(seeds[7], (H, DH, DH), DH ** -0.5, 0.375, ((0, 8),))
    return {"queries": queries, "key_tokens": key_tokens, "values": values, "out_grad": out_grad, "learn_rates": learn_rates, "w_gate": w_gate, "w_up": w_up, "w_down": w_down}


def silu_slope(pre_act):
    sigmoid_val = jax.nn.sigmoid(pre_act)
    return sigmoid_val * (1.0 + pre_act * (1.0 - sigmoid_val))

def silu_curve(pre_act):
    sigmoid_val = jax.nn.sigmoid(pre_act)
    return sigmoid_val * (1.0 - sigmoid_val) * (2.0 + pre_act * (1.0 - 2.0 * sigmoid_val))

def key_forward(key_rows, scaled, gate_mat, up_mat, down_mat):
    gate_pre = jnp.dot(key_rows, gate_mat, preferred_element_type=jnp.float32)
    up_pre = jnp.dot(key_rows, up_mat, preferred_element_type=jnp.float32)
    gate_act = jax.nn.silu(gate_pre)
    hidden = (gate_act * up_pre).astype(jnp.bfloat16)
    key_dhid = jnp.dot(scaled, down_mat.T, preferred_element_type=jnp.float32)
    grad_gate = (key_dhid * up_pre * silu_slope(gate_pre)).astype(jnp.bfloat16)
    grad_upper = (key_dhid * gate_act).astype(jnp.bfloat16)
    delta_gate = jnp.dot(key_rows.T, grad_gate, preferred_element_type=jnp.float32)
    delta_up = jnp.dot(key_rows.T, grad_upper, preferred_element_type=jnp.float32)
    delta_down = jnp.dot(hidden.T, scaled, preferred_element_type=jnp.float32)
    stored = (gate_pre, up_pre, hidden, key_dhid, grad_gate, grad_upper)
    return ((delta_gate, delta_up, delta_down), stored)

def query_side(query_rows, out_rows, fresh_gate, fresh_up, fresh_down):
    gate_pre = jnp.dot(query_rows, fresh_gate, preferred_element_type=jnp.float32)
    up_pre = jnp.dot(query_rows, fresh_up, preferred_element_type=jnp.float32)
    gate_act = jax.nn.silu(gate_pre)
    hidden = (gate_act * up_pre).astype(jnp.bfloat16)
    query_dhid = jnp.dot(out_rows, fresh_down.T, preferred_element_type=jnp.float32)
    grad_gate = (query_dhid * up_pre * silu_slope(gate_pre)).astype(jnp.bfloat16)
    grad_upper = (query_dhid * gate_act).astype(jnp.bfloat16)
    query_grad = jnp.dot(grad_gate, fresh_gate.T, preferred_element_type=jnp.float32)
    query_grad = query_grad + jnp.dot(grad_upper, fresh_up.T, preferred_element_type=jnp.float32)
    sum_gate = jnp.dot(query_rows.T, grad_gate, preferred_element_type=jnp.float32)
    sum_up = jnp.dot(query_rows.T, grad_upper, preferred_element_type=jnp.float32)
    sum_down = jnp.dot(hidden.T, out_rows, preferred_element_type=jnp.float32)
    return (query_grad.astype(jnp.bfloat16), (sum_gate, sum_up, sum_down))

def key_back(key_rows, scaled, rate_col, gate_mat, up_mat, down_mat, stored, adj_gate, adj_up, adj_down):
    gate_pre, up_pre, hidden, key_dhid, grad_gate, grad_upper = stored
    back_dgate = jnp.dot(key_rows, adj_gate, preferred_element_type=jnp.float32)
    back_dup = jnp.dot(key_rows, adj_up, preferred_element_type=jnp.float32)
    back_hidden = jnp.dot(scaled, adj_down.T, preferred_element_type=jnp.float32)
    back_scaled = jnp.dot(hidden, adj_down, preferred_element_type=jnp.float32)
    gate_act = jax.nn.silu(gate_pre)
    gate_slope = silu_slope(gate_pre)
    back_dhid = (back_dgate * up_pre * gate_slope + back_dup * gate_act).astype(jnp.bfloat16)
    back_gate = (back_dgate * key_dhid * up_pre * silu_curve(gate_pre) + (back_dup * key_dhid + back_hidden * up_pre) * gate_slope).astype(jnp.bfloat16)
    back_upper = (back_dgate * key_dhid * gate_slope + back_hidden * gate_act).astype(jnp.bfloat16)
    key_grad = jnp.dot(grad_gate, adj_gate.T, preferred_element_type=jnp.float32)
    key_grad = key_grad + jnp.dot(grad_upper, adj_up.T, preferred_element_type=jnp.float32)
    key_grad = key_grad + jnp.dot(back_gate, gate_mat.T, preferred_element_type=jnp.float32)
    key_grad = key_grad + jnp.dot(back_upper, up_mat.T, preferred_element_type=jnp.float32)
    value_grad = rate_col[:, None] * (back_scaled + jnp.dot(back_dhid, down_mat, preferred_element_type=jnp.float32))
    return (key_grad.astype(jnp.bfloat16), value_grad.astype(jnp.bfloat16))

def reference(queries, key_tokens, values, out_grad, learn_rates, w_gate, w_up, w_down):
    update_scale = 1.0 / math.sqrt(DH * TOKENS)
    query_list = []
    key_list = []
    value_list = []
    for head_index in range(H):
        first = head_index * DH
        key_rows = key_tokens[:, first:first + DH]
        query_rows = queries[:, first:first + DH]
        out_rows = out_grad[:, first:first + DH]
        rate_col = learn_rates[:, head_index]
        scaled = (rate_col[:, None] * values[:, first:first + DH].astype(jnp.float32)).astype(jnp.bfloat16)
        deltas, stored = key_forward(key_rows, scaled, w_gate[head_index], w_up[head_index], w_down[head_index])
        fresh_gate = (w_gate[head_index].astype(jnp.float32) + update_scale * deltas[0]).astype(jnp.bfloat16)
        fresh_up = (w_up[head_index].astype(jnp.float32) + update_scale * deltas[1]).astype(jnp.bfloat16)
        fresh_down = (w_down[head_index].astype(jnp.float32) + update_scale * deltas[2]).astype(jnp.bfloat16)
        query_grad, sums = query_side(query_rows, out_rows, fresh_gate, fresh_up, fresh_down)
        adj_gate = (update_scale * sums[0]).astype(jnp.bfloat16)
        adj_up = (update_scale * sums[1]).astype(jnp.bfloat16)
        adj_down = (update_scale * sums[2]).astype(jnp.bfloat16)
        key_grad, value_grad = key_back(key_rows, scaled, rate_col, w_gate[head_index], w_up[head_index], w_down[head_index], stored, adj_gate, adj_up, adj_down)
        query_list.append(query_grad)
        key_list.append(key_grad)
        value_list.append(value_grad)
    return (jnp.concatenate(query_list, axis=1), jnp.concatenate(key_list, axis=1), jnp.concatenate(value_list, axis=1))
```

```python
import functools
import math

import jax
import jax.numpy as jnp
from jax import lax
from jax.experimental import pallas as pl
from jax.experimental.pallas import tpu as pltpu
from jax.sharding import PartitionSpec as P

DH = 256
NX, NZ, NY, NC = 4, 8, 4, 2
NH = NY * NC
ROWS = 128
ALL = NH * ROWS
PART = 3 * DH // NX
CHUNK = 256
MESH = pl.DeviceIdType.MESH
F32 = jnp.float32
BF16 = jnp.bfloat16


def mm(a, b):
    return jnp.dot(a, b, preferred_element_type=F32)


def mm_rt(a, b):
    return lax.dot_general(a, b, (((1,), (1,)), ((), ())), preferred_element_type=F32)


def mm_lt(a, b):
    return lax.dot_general(a, b, (((0,), (0,)), ((), ())), preferred_element_type=F32)


def kernel(
    scale,
    q_in, k_in, v_in, o_in, lr_in, wg_in, wu_in, wd_in,
    gq_out, gk_out, gv_out,
    buf, lr, w, acc, pb, rx, zf, zs, rz, full,
    gate, upper, dhid, hid, dgate, dup, scaled, stage,
    in_send, in_recv, in_loc, w_sem, lr_sem,
    xs, xr, zsd, zrv, azs, azr, axs, axr,
    out_send, out_recv, out_loc,
):
    tok, me = lax.axis_index("tok"), lax.axis_index("head")
    x, z = tok // NZ, tok % NZ
    y, c = me // NC, me % NC
    ins = (k_in, v_in, q_in, o_in)
    outs = (gq_out, gk_out, gv_out)

    ypeers = [(2, 0), (2, 1), (1, 0), (3, 0), (1, 1), (3, 1), (0, 1)]
    hpeers = [lax.rem(y + dy, NY) * NC + lax.rem(c + dc, NC) for dy, dc in ypeers]
    xpeers = [lax.rem(x + d, NX) for d in (2, 1, 3)]
    zds = (4, 3, 5, 2, 6, 1, 7)
    zpeers = [lax.rem(z + d, NZ) for d in zds]

    def xdev(px):
        return (px * NZ + z, me)

    def zdev(pz):
        return (x * NZ + pz, me)

    barrier = pltpu.get_barrier_semaphore()
    for p in hpeers:
        pl.semaphore_signal(barrier, inc=1, device_id=(tok, p), device_id_type=MESH)
    for p in xpeers:
        pl.semaphore_signal(barrier, inc=1, device_id=xdev(p), device_id_type=MESH)
    for p in zpeers:
        pl.semaphore_signal(barrier, inc=1, device_id=zdev(p), device_id_type=MESH)

    loc = []

    def cols(p, h):
        return pl.ds(pl.multiple_of(p * (2 * DH) + h * DH, DH), DH)

    def rows_of(p):
        return pl.ds(pl.multiple_of(p * ROWS, ROWS), ROWS)

    def local_in(a, h):
        cp = pltpu.make_async_copy(ins[a].at[:, cols(me, h)], buf.at[a, h, rows_of(me)], in_loc.at[a, h])
        cp.start()
        return cp

    wcp = []
    for h in range(2):
        for m, ref in enumerate((wg_in, wu_in, wd_in)):
            cp = pltpu.make_async_copy(ref.at[h], w.at[h, pl.ds(m * DH, DH)], w_sem.at[h, m])
            cp.start()
            wcp.append(cp)
    lcp = pltpu.make_async_copy(lr_in, lr, lr_sem)
    lcp.start()
    locals_in = {(a, h): local_in(a, h) for h in range(2) for a in range(4)}

    pl.semaphore_wait(barrier, len(hpeers) + len(xpeers) + len(zpeers))

    def send_in(a, h):
        for p in hpeers:
            pltpu.make_async_remote_copy(
                src_ref=ins[a].at[:, cols(p, h)],
                dst_ref=buf.at[a, h, rows_of(me)],
                send_sem=in_send.at[a, h],
                recv_sem=in_recv.at[a, h],
                device_id=(tok, p),
                device_id_type=MESH,
            ).start()

    def wait_bytes(ref, sem):
        pltpu.make_async_copy(ref, ref, sem).wait()

    def wait_in(a, h):
        locals_in[(a, h)].wait()
        wait_bytes(buf.at[a, h, pl.ds(0, ALL - ROWS)], in_recv.at[a, h])

    def key_forward(h):
        acc[0, h] = jnp.zeros((3 * DH, DH), F32)

        def step(j, carry):
            rows = pl.ds(pl.multiple_of(j * CHUNK, CHUNK), CHUNK)
            kr = buf[0, h, rows]
            sc = (lr[rows, h:h + 1] * buf[1, h, rows].astype(F32)).astype(BF16)
            scaled[h, rows] = sc
            gp = mm(kr, w[h, 0:DH])
            up = mm(kr, w[h, DH:2 * DH])
            kd = mm_rt(sc, w[h, 2 * DH:3 * DH])
            s = jax.nn.sigmoid(gp)
            act = gp * s
            slope = s * (1.0 + gp * (1.0 - s))
            hd = (act * up).astype(BF16)
            dg = (kd * up * slope).astype(BF16)
            du = (kd * act).astype(BF16)
            gate[h, rows] = gp
            upper[h, rows] = up
            dhid[h, rows] = kd
            hid[h, rows] = hd
            dgate[h, rows] = dg
            dup[h, rows] = du
            acc[0, h, 0:DH] += mm_lt(kr, dg)
            acc[0, h, DH:2 * DH] += mm_lt(kr, du)
            acc[0, h, 2 * DH:3 * DH] += mm_lt(hd, sc)
            return carry

        lax.fori_loop(0, ALL // CHUNK, step, 0)

    def part(p):
        return pl.ds(pl.multiple_of(p * PART, 16), PART)

    def rs_x_start(f, h):
        pb[f, h] = acc[f, h].astype(BF16)
        for i, p in enumerate(xpeers):
            pltpu.make_async_remote_copy(
                src_ref=pb.at[f, h, part(p)],
                dst_ref=rx.at[f, h, i],
                send_sem=xs.at[f, h],
                recv_sem=xr.at[f, h],
                device_id=xdev(p),
                device_id_type=MESH,
            ).start()

    def prow(p):
        return pl.multiple_of((p // 2) * 48, 16)

    def pcol(p):
        return pl.ds(pl.multiple_of((p % 2) * 128, 128), 128)

    def rs_x_finish(f, h):
        wait_bytes(rx.at[f, h], xr.at[f, h])
        total = acc[f, h, part(x)]
        for i in range(3):
            total = total + rx[f, h, i].astype(F32)
        zf[f, h] = total
        zs[f, h] = total.astype(BF16)
        for i, p in enumerate(zpeers):
            pltpu.make_async_remote_copy(
                src_ref=zs.at[f, h, pl.ds(prow(p), 48), pcol(p)],
                dst_ref=rz.at[f, h, i],
                send_sem=zsd.at[f, h],
                recv_sem=zrv.at[f, h],
                device_id=zdev(p),
                device_id_type=MESH,
            ).start()

    def rs_z_finish(f, h):
        wait_bytes(rz.at[f, h], zrv.at[f, h])
        total = zf[f, h, pl.ds(prow(z), 48), pcol(z)]
        for i in range(7):
            total = total + rz[f, h, i].astype(F32)
        own = pl.ds(pl.multiple_of(x * PART + prow(z), 16), 48)
        total = total * scale
        if f == 0:
            total = w[h, own, pcol(z)].astype(F32) + total
        full[f, h, own, pcol(z)] = total.astype(BF16)
        for p in zpeers:
            pltpu.make_async_remote_copy(
                src_ref=full.at[f, h, own, pcol(z)],
                dst_ref=full.at[f, h, own, pcol(z)],
                send_sem=azs.at[f, h],
                recv_sem=azr.at[f, h],
                device_id=zdev(p),
                device_id_type=MESH,
            ).start()

    def ag_z_finish(f, h):
        wait_bytes(rz.at[f, h], azr.at[f, h])
        for p in xpeers:
            pltpu.make_async_remote_copy(
                src_ref=full.at[f, h, part(x)],
                dst_ref=full.at[f, h, part(x)],
                send_sem=axs.at[f, h],
                recv_sem=axr.at[f, h],
                device_id=xdev(p),
                device_id_type=MESH,
            ).start()

    def ag_x_finish(f, h):
        wait_bytes(rx.at[f, h], axr.at[f, h])

    def send_out(a, h, yy, own_chip):
        def remote(p):
            pltpu.make_async_remote_copy(
                src_ref=stage.at[a, h, rows_of(p)],
                dst_ref=outs[a].at[:, cols(me, h)],
                send_sem=out_send.at[a, h],
                recv_sem=out_recv.at[a, h],
                device_id=(tok, p),
                device_id_type=MESH,
            ).start()

        @pl.when(jnp.logical_not(own_chip))
        def _():
            for cc in range(NC):
                remote(yy * NC + cc)

        @pl.when(own_chip)
        def _():
            remote(y * NC + (1 - c))
            pltpu.make_async_copy(
                stage.at[a, h, rows_of(me)], outs[a].at[:, cols(me, h)], out_loc.at[a, h]
            ).start()

    def query_side(h):
        acc[1, h] = jnp.zeros((3 * DH, DH), F32)

        def step(j, carry):
            yy = lax.rem(y + 1 + j, NY)
            rows = pl.ds(pl.multiple_of(yy * CHUNK, CHUNK), CHUNK)
            qr = buf[2, h, rows]
            orr = buf[3, h, rows]
            ng = full[0, h, 0:DH]
            nu = full[0, h, DH:2 * DH]
            gp = mm(qr, ng)
            up = mm(qr, nu)
            qd = mm_rt(orr, full[0, h, 2 * DH:3 * DH])
            s = jax.nn.sigmoid(gp)
            act = gp * s
            slope = s * (1.0 + gp * (1.0 - s))
            hd = (act * up).astype(BF16)
            dg = (qd * up * slope).astype(BF16)
            du = (qd * act).astype(BF16)
            stage[0, h, rows] = (mm_rt(dg, ng) + mm_rt(du, nu)).astype(BF16)
            send_out(0, h, yy, j == NY - 1)
            acc[1, h, 0:DH] += mm_lt(qr, dg)
            acc[1, h, DH:2 * DH] += mm_lt(qr, du)
            acc[1, h, 2 * DH:3 * DH] += mm_lt(hd, orr)
            return carry

        lax.fori_loop(0, NY, step, 0)

    def key_back(h):
        def step(j, carry):
            yy = lax.rem(y + 1 + j, NY)
            rows = pl.ds(pl.multiple_of(yy * CHUNK, CHUNK), CHUNK)
            kr = buf[0, h, rows]
            ag = full[1, h, 0:DH]
            au = full[1, h, DH:2 * DH]
            ad = full[1, h, 2 * DH:3 * DH]
            bdg = mm(kr, ag)
            bdu = mm(kr, au)
            bh = mm_rt(scaled[h, rows], ad)
            gp = gate[h, rows]
            up = upper[h, rows]
            kd = dhid[h, rows]
            s = jax.nn.sigmoid(gp)
            act = gp * s
            slope = s * (1.0 + gp * (1.0 - s))
            curve = s * (1.0 - s) * (2.0 + gp * (1.0 - 2.0 * s))
            bdh = (bdg * up * slope + bdu * act).astype(BF16)
            bg = (bdg * kd * up * curve + (bdu * kd + bh * up) * slope).astype(BF16)
            bu = (bdg * kd * slope + bh * act).astype(BF16)
            kg = mm_rt(dgate[h, rows], ag) + mm_rt(dup[h, rows], au)
            kg = kg + mm_rt(bg, w[h, 0:DH]) + mm_rt(bu, w[h, DH:2 * DH])
            stage[1, h, rows] = kg.astype(BF16)
            send_out(1, h, yy, j == NY - 1)
            vg = mm(hid[h, rows], ad) + mm(bdh, w[h, 2 * DH:3 * DH])
            stage[2, h, rows] = (lr[rows, h:h + 1] * vg).astype(BF16)
            send_out(2, h, yy, j == NY - 1)
            return carry

        lax.fori_loop(0, NY, step, 0)

    for h in range(2):
        send_in(0, h)
        send_in(1, h)
    for cp in wcp:
        cp.wait()
    lcp.wait()

    wait_in(0, 0)
    wait_in(1, 0)
    send_in(2, 0)
    send_in(3, 0)
    key_forward(0)
    rs_x_start(0, 0)
    rs_x_finish(0, 0)
    wait_in(0, 1)
    wait_in(1, 1)
    send_in(2, 1)
    send_in(3, 1)
    key_forward(1)
    rs_x_start(0, 1)
    rs_z_finish(0, 0)
    ag_z_finish(0, 0)
    rs_x_finish(0, 1)
    rs_z_finish(0, 1)
    ag_z_finish(0, 1)
    ag_x_finish(0, 0)
    wait_in(2, 0)
    wait_in(3, 0)
    query_side(0)
    rs_x_start(1, 0)
    ag_x_finish(0, 1)
    rs_x_finish(1, 0)
    wait_in(2, 1)
    wait_in(3, 1)
    query_side(1)
    rs_x_start(1, 1)
    rs_z_finish(1, 0)
    ag_z_finish(1, 0)
    rs_x_finish(1, 1)
    rs_z_finish(1, 1)
    ag_x_finish(1, 0)
    key_back(0)
    ag_z_finish(1, 1)
    ag_x_finish(1, 1)
    key_back(1)

    for h in range(2):
        for a in range(4):
            wait_bytes(buf.at[a, h, pl.ds(0, ALL - ROWS)], in_send.at[a, h])
        for f in range(2):
            wait_bytes(rx.at[f, h], xs.at[f, h])
            wait_bytes(rz.at[f, h], zsd.at[f, h])
            wait_bytes(rz.at[f, h], azs.at[f, h])
            wait_bytes(rx.at[f, h], axs.at[f, h])
        for a in range(3):
            wait_bytes(stage.at[a, h, pl.ds(0, ALL - ROWS)], out_send.at[a, h])
            wait_bytes(stage.at[a, h, pl.ds(0, ALL - ROWS)], out_recv.at[a, h])
            wait_bytes(stage.at[a, h, pl.ds(0, ROWS)], out_loc.at[a, h])


def body(queries, key_tokens, values, out_grad, learn_rates, w_gate, w_up, w_down):
    scale = 1.0 / math.sqrt(DH * ALL * NX * NZ)
    dma = pltpu.SemaphoreType.DMA
    out = jax.ShapeDtypeStruct(queries.shape, BF16)
    return pl.pallas_call(
        functools.partial(kernel, scale),
        out_shape=(out, out, out),
        in_specs=[pl.BlockSpec(memory_space=pl.ANY)] * 8,
        out_specs=[pl.BlockSpec(memory_space=pl.ANY)] * 3,
        scratch_shapes=[
            pltpu.VMEM((4, 2, ALL, DH), BF16),
            pltpu.VMEM((ALL, 2), F32),
            pltpu.VMEM((2, 3 * DH, DH), BF16),
            pltpu.VMEM((2, 2, 3 * DH, DH), F32),
            pltpu.VMEM((2, 2, 3 * DH, DH), BF16),
            pltpu.VMEM((2, 2, NX - 1, PART, DH), BF16),
            pltpu.VMEM((2, 2, PART, DH), F32),
            pltpu.VMEM((2, 2, PART, DH), BF16),
            pltpu.VMEM((2, 2, NZ - 1, 48, 128), BF16),
            pltpu.VMEM((2, 2, 3 * DH, DH), BF16),
            pltpu.VMEM((2, ALL, DH), F32),
            pltpu.VMEM((2, ALL, DH), F32),
            pltpu.VMEM((2, ALL, DH), F32),
            pltpu.VMEM((2, ALL, DH), BF16),
            pltpu.VMEM((2, ALL, DH), BF16),
            pltpu.VMEM((2, ALL, DH), BF16),
            pltpu.VMEM((2, ALL, DH), BF16),
            pltpu.VMEM((3, 2, ALL, DH), BF16),
            dma((4, 2)), dma((4, 2)), dma((4, 2)), dma((2, 3)), dma,
            dma((2, 2)), dma((2, 2)), dma((2, 2)), dma((2, 2)),
            dma((2, 2)), dma((2, 2)), dma((2, 2)), dma((2, 2)),
            dma((3, 2)), dma((3, 2)), dma((3, 2)),
        ],
        compiler_params=pltpu.CompilerParams(
            collective_id=0, has_side_effects=True, vmem_limit_bytes=48 << 20
        ),
    )(queries, key_tokens, values, out_grad, learn_rates, w_gate, w_up, w_down)


def solution(mesh):
    tokens = P(("tok", "head"), None)
    heads = P("head", None, None)
    return jax.shard_map(
        body,
        mesh=mesh,
        in_specs=(tokens, tokens, tokens, tokens, P("tok", "head"), heads, heads, heads),
        out_specs=(tokens, tokens, tokens),
        check_vma=False,
    )
```

```python
import functools
import math

import jax
import jax.numpy as jnp
from jax import lax
from jax.experimental import pallas as pl
from jax.experimental.pallas import tpu as pltpu
from jax.sharding import PartitionSpec as P

DH = 256
NX, NZ, NY, NC = 4, 8, 4, 2
NH = NY * NC
ROWS = 128
ALL = NH * ROWS
PART = DH // NX
ZROWS, ZCOLS = 16, 128
EIGHTH = DH // NZ
CHUNK = 256
MESH = pl.DeviceIdType.MESH
F32 = jnp.float32
BF16 = jnp.bfloat16


def mm(a, b):
    return jnp.dot(a, b, preferred_element_type=F32)


def mm_rt(a, b):
    return lax.dot_general(a, b, (((1,), (1,)), ((), ())), preferred_element_type=F32)


def mm_lt(a, b):
    return lax.dot_general(a, b, (((0,), (0,)), ((), ())), preferred_element_type=F32)


def kernel(
    scale,
    q_in, k_in, v_in, o_in, lr_in, wg_in, wu_in, wd_in,
    gq_out, gk_out, gv_out,
    buf, lrc, lrow, lsend, lq, lfin, wz, w, acc, pb, rx, zf, zs, rz, full,
    gate, upper, dhid, hid, dgate, dup, scaled, stage,
    in_send, in_recv, in_loc, w_sem, lr_sem, w1s, w1r, w2s, w2r, l1s, l1r, l2s, l2r,
    xs, xr, zsd, zrv, azs, azr, axs, axr,
    out_send, out_recv, out_loc,
):
    tok, me = lax.axis_index("tok"), lax.axis_index("head")
    x, z = tok // NZ, tok % NZ
    y, c = me // NC, me % NC
    ins = (k_in, v_in, q_in, o_in)
    outs = (gq_out, gk_out, gv_out)

    spots = [(1, 0), (3, 0), (1, 1), (3, 1), (2, 0), (2, 1), (0, 1)]
    chip = (y, x)
    line = (me, x * NC + c)
    lpeers = [
        [(lax.rem(chip[g] + dp, NY) * NC + lax.rem(c + dc, NC)) for dp, dc in spots] for g in range(2)
    ]
    cpos = (x, y)
    cpeers = [[lax.rem(cpos[g] + d, NX) for d in (2, 1, 3)] for g in range(2)]
    zpeers = [lax.rem(z + d, NZ) for d in (4, 3, 5, 2, 6, 1, 7)]

    def ldev(g, p):
        return (tok, p) if g == 0 else ((p // NC) * NZ + z, y * NC + p % NC)

    def cdev(g, p):
        return (p * NZ + z, me) if g == 0 else (tok, p * NC + c)

    def zdev(pz):
        return (x * NZ + pz, me)

    barrier = pltpu.get_barrier_semaphore()
    greet = [ldev(0, p) for p in lpeers[0]] + [ldev(1, p) for p in lpeers[1][:-1]] + [zdev(p) for p in zpeers]
    for p in greet:
        pl.semaphore_signal(barrier, inc=1, device_id=p, device_id_type=MESH)

    def cols(p, h):
        return pl.ds(pl.multiple_of(p * (2 * DH) + h * DH, DH), DH)

    def rows_of(p):
        return pl.ds(pl.multiple_of(p * ROWS, ROWS), ROWS)

    def local_in(a, h):
        cp = pltpu.make_async_copy(ins[a].at[:, cols(line[h], h)], buf.at[a, h, rows_of(line[h])], in_loc.at[a, h])
        cp.start()
        return cp

    w_in = (wg_in, wu_in, wd_in)
    eighth = pl.ds(pl.multiple_of(z * EIGHTH, EIGHTH), EIGHTH)
    diagonal = x == y
    wcp = []
    for m in range(3):
        wcp.append(pltpu.make_async_copy(w_in[m].at[0], w.at[0, pl.ds(m * DH, DH)], w_sem.at[0, m]))
    lcp = pltpu.make_async_copy(lr_in, lrow, lr_sem)
    lcp.start()
    for cp in wcp:
        cp.start()
    locals_in = {(a, h): local_in(a, h) for h in range(2) for a in range(4)}
    lcp.wait()
    for i in range(NY):
        lsend[i] = jnp.broadcast_to(lrow[1:2, i * CHUNK:(i + 1) * CHUNK], (8, CHUNK))
    lq[y] = lsend[y]

    pl.semaphore_wait(barrier, len(greet))

    def column(row):
        return jnp.broadcast_to(row, (128, CHUNK)).T

    def weights_first():
        @pl.when(diagonal)
        def _():
            for m in range(3):
                pltpu.make_async_copy(w_in[m].at[1, eighth], wz.at[z, m], w_sem.at[1, m]).start()
                for p in cpeers[1]:
                    pltpu.make_async_remote_copy(
                        src_ref=w_in[m].at[1, eighth],
                        dst_ref=wz.at[z, m],
                        send_sem=w1s,
                        recv_sem=w1r,
                        device_id=cdev(1, p),
                        device_id_type=MESH,
                    ).start()

        for p in cpeers[1]:
            pltpu.make_async_remote_copy(
                src_ref=lsend.at[p],
                dst_ref=lq.at[y],
                send_sem=l1s,
                recv_sem=l1r,
                device_id=cdev(1, p),
                device_id_type=MESH,
            ).start()

    def weights_second():
        @pl.when(diagonal)
        def _():
            for m in range(3):
                wait_bytes(wz.at[0, m], w_sem.at[1, m])

        @pl.when(jnp.logical_not(diagonal))
        def _():
            wait_bytes(wz.at[0], w1r)

        for p in zpeers:
            pltpu.make_async_remote_copy(
                src_ref=wz.at[z],
                dst_ref=wz.at[z],
                send_sem=w2s,
                recv_sem=w2r,
                device_id=zdev(p),
                device_id_type=MESH,
            ).start()
        wait_bytes(lq.at[pl.ds(0, 3)], l1r)
        for p in cpeers[0]:
            pltpu.make_async_remote_copy(
                src_ref=lq.at[p],
                dst_ref=lfin.at[x],
                send_sem=l2s,
                recv_sem=l2r,
                device_id=cdev(0, p),
                device_id_type=MESH,
            ).start()
        lfin[x] = lq[x]
        for i in range(NY):
            lrc[0, pl.ds(i * CHUNK, CHUNK)] = column(lrow[0:1, i * CHUNK:(i + 1) * CHUNK])

    def weights_third():
        wait_bytes(wz.at[pl.ds(0, NZ - 1)], w2r)
        wait_bytes(lq.at[pl.ds(0, 3)], l2r)
        for i in range(NZ):
            for m in range(3):
                w[1, pl.ds(m * DH + i * EIGHTH, EIGHTH)] = wz[i, m]
        for i in range(NX):
            lrc[1, pl.ds(i * CHUNK, CHUNK)] = column(lfin[i, 0:1])

    def rates(h, rows):
        col = lrc[h, rows]
        return jnp.concatenate([col, col], axis=1)

    def send_in(a, h, which=range(7)):
        for p in [lpeers[h][i] for i in which]:
            pltpu.make_async_remote_copy(
                src_ref=ins[a].at[:, cols(p, h)],
                dst_ref=buf.at[a, h, rows_of(line[h])],
                send_sem=in_send.at[a, h],
                recv_sem=in_recv.at[a, h, chip[h]],
                device_id=ldev(h, p),
                device_id_type=MESH,
            ).start()

    def wait_bytes(ref, sem):
        pltpu.make_async_copy(ref, ref, sem).wait()

    def wait_in(a, h, off):
        cc = lax.rem(chip[h] + off, NY)
        if off == 0:
            locals_in[(a, h)].wait()
            wait_bytes(buf.at[a, h, pl.ds(0, ROWS)], in_recv.at[a, h, cc])
        else:
            wait_bytes(buf.at[a, h, pl.ds(0, CHUNK)], in_recv.at[a, h, cc])

    def silu_parts(gp):
        s = 0.5 * jnp.tanh(0.5 * gp) + 0.5
        act = gp * s
        rest = 1.0 - s
        return s, act, rest, s + act * rest

    def key_forward(h, off):
        wait_in(0, h, off)
        wait_in(1, h, off)
        cc = lax.rem(chip[h] + off, NY)
        rows = pl.ds(pl.multiple_of(cc * CHUNK, CHUNK), CHUNK)
        kr = buf[0, h, rows]
        sc = (rates(h, rows) * buf[1, h, rows].astype(F32)).astype(BF16)
        scaled[h, rows] = sc
        gp = mm(kr, w[h, 0:DH])
        up = mm(kr, w[h, DH:2 * DH])
        kd = mm_rt(sc, w[h, 2 * DH:3 * DH])
        s, act, rest, slope = silu_parts(gp)
        hd = (act * up).astype(BF16)
        dg = (kd * up * slope).astype(BF16)
        du = (kd * act).astype(BF16)
        gate[h, rows] = gp
        upper[h, rows] = up
        dhid[h, rows] = kd
        hid[h, rows] = hd
        dgate[h, rows] = dg
        dup[h, rows] = du
        for m, term in enumerate((mm_lt(kr, dg), mm_lt(kr, du), mm_lt(hd, sc))):
            mat = pl.ds(m * DH, DH)
            acc[0, h, mat] = term if off == 0 else acc[0, h, mat] + term

    def part(m, p):
        return pl.ds(pl.multiple_of(m * DH + p * PART, PART), PART)

    def zrow(p):
        return pl.multiple_of((p // 2) * ZROWS, ZROWS)

    def zcol(p):
        return pl.ds(pl.multiple_of((p % 2) * ZCOLS, ZCOLS), ZCOLS)

    def rs_x_start(f, h, m):
        mat = pl.ds(m * DH, DH)
        pb[f, h, mat] = acc[f, h, mat].astype(BF16)
        for i, p in enumerate(cpeers[h]):
            pltpu.make_async_remote_copy(
                src_ref=pb.at[f, h, part(m, p)],
                dst_ref=rx.at[f, h, m, i],
                send_sem=xs.at[f, h, m],
                recv_sem=xr.at[f, h, m],
                device_id=cdev(h, p),
                device_id_type=MESH,
            ).start()

    def rs_x_finish(f, h, m):
        wait_bytes(rx.at[f, h, m], xr.at[f, h, m])
        total = acc[f, h, part(m, cpos[h])]
        for i in range(NX - 1):
            total = total + rx[f, h, m, i].astype(F32)
        zf[f, h, m] = total
        zs[f, h, m] = total.astype(BF16)
        for i, p in enumerate(zpeers):
            pltpu.make_async_remote_copy(
                src_ref=zs.at[f, h, m, pl.ds(zrow(p), ZROWS), zcol(p)],
                dst_ref=rz.at[f, h, m, i],
                send_sem=zsd.at[f, h, m],
                recv_sem=zrv.at[f, h, m],
                device_id=zdev(p),
                device_id_type=MESH,
            ).start()

    def rs_z_finish(f, h, m):
        wait_bytes(rz.at[f, h, m], zrv.at[f, h, m])
        total = zf[f, h, m, pl.ds(zrow(z), ZROWS), zcol(z)]
        for i in range(NZ - 1):
            total = total + rz[f, h, m, i].astype(F32)
        own = pl.ds(pl.multiple_of(m * DH + cpos[h] * PART + zrow(z), ZROWS), ZROWS)
        total = total * scale
        if f == 0:
            total = w[h, own, zcol(z)].astype(F32) + total
        full[f, h, own, zcol(z)] = total.astype(BF16)
        for p in zpeers:
            pltpu.make_async_remote_copy(
                src_ref=full.at[f, h, own, zcol(z)],
                dst_ref=full.at[f, h, own, zcol(z)],
                send_sem=azs.at[f, h, m],
                recv_sem=azr.at[f, h, m],
                device_id=zdev(p),
                device_id_type=MESH,
            ).start()

    def ag_z_finish(f, h, m):
        wait_bytes(rz.at[f, h, m], azr.at[f, h, m])
        for p in cpeers[h]:
            pltpu.make_async_remote_copy(
                src_ref=full.at[f, h, part(m, cpos[h])],
                dst_ref=full.at[f, h, part(m, cpos[h])],
                send_sem=axs.at[f, h, m],
                recv_sem=axr.at[f, h, m],
                device_id=cdev(h, p),
                device_id_type=MESH,
            ).start()

    def ag_x_finish(f, h, m):
        wait_bytes(rx.at[f, h, m], axr.at[f, h, m])

    def send_out(a, h, cc, own_chip):
        def remote(p):
            pltpu.make_async_remote_copy(
                src_ref=stage.at[a, h, rows_of(p)],
                dst_ref=outs[a].at[:, cols(line[h], h)],
                send_sem=out_send.at[a, h],
                recv_sem=out_recv.at[a, h],
                device_id=ldev(h, p),
                device_id_type=MESH,
            ).start()

        @pl.when(jnp.logical_not(own_chip))
        def _():
            for core in range(NC):
                remote(cc * NC + core)

        @pl.when(own_chip)
        def _():
            remote(chip[h] * NC + (1 - c))
            pltpu.make_async_copy(
                stage.at[a, h, rows_of(line[h])], outs[a].at[:, cols(line[h], h)], out_loc.at[a, h]
            ).start()

    def chunk_of(h, j):
        cc = lax.rem(chip[h] + 2 + j + j // 2 + 2 * (j // 3), NY)
        return cc, pl.ds(pl.multiple_of(cc * CHUNK, CHUNK), CHUNK)

    def query_side(h):
        acc[1, h] = jnp.zeros((3 * DH, DH), F32)

        def step(j, carry):
            yy, rows = chunk_of(h, j)
            qr = buf[2, h, rows]
            orr = buf[3, h, rows]
            ng = full[0, h, 0:DH]
            nu = full[0, h, DH:2 * DH]
            gp = mm(qr, ng)
            up = mm(qr, nu)
            qd = mm_rt(orr, full[0, h, 2 * DH:3 * DH])
            s, act, rest, slope = silu_parts(gp)
            hd = (act * up).astype(BF16)
            dg = (qd * up * slope).astype(BF16)
            du = (qd * act).astype(BF16)
            stage[0, h, rows] = (mm_rt(dg, ng) + mm_rt(du, nu)).astype(BF16)
            acc[1, h, 0:DH] += mm_lt(qr, dg)
            acc[1, h, DH:2 * DH] += mm_lt(qr, du)
            acc[1, h, 2 * DH:3 * DH] += mm_lt(hd, orr)
            return carry

        lax.fori_loop(0, NY, step, 0)

    def back(h, j):
        yy, rows = chunk_of(h, j)
        kr = buf[0, h, rows]
        ag = full[1, h, 0:DH]
        au = full[1, h, DH:2 * DH]
        ad = full[1, h, 2 * DH:3 * DH]
        bdg = mm(kr, ag)
        bdu = mm(kr, au)
        bh = mm_rt(scaled[h, rows], ad)
        gp = gate[h, rows]
        up = upper[h, rows]
        kd = dhid[h, rows]
        s, act, rest, slope = silu_parts(gp)
        twice = s + s
        curve = rest * (twice + act * (1.0 - twice))
        bdh = (bdg * up * slope + bdu * act).astype(BF16)
        bg = (bdg * kd * up * curve + (bdu * kd + bh * up) * slope).astype(BF16)
        bu = (bdg * kd * slope + bh * act).astype(BF16)
        kg = mm_rt(dgate[h, rows], ag) + mm_rt(dup[h, rows], au)
        kg = kg + mm_rt(bg, w[h, 0:DH]) + mm_rt(bu, w[h, DH:2 * DH])
        stage[1, h, rows] = kg.astype(BF16)
        send_out(1, h, yy, j == NY - 1)
        vg = mm(hid[h, rows], ad) + mm(bdh, w[h, 2 * DH:3 * DH])
        stage[2, h, rows] = (rates(h, rows) * vg).astype(BF16)
        send_out(2, h, yy, j == NY - 1)

    def key_back():
        def step(j, carry):
            back(0, j)
            back(1, j)
            return carry

        lax.fori_loop(0, NY, step, 0)

    def send_query(h):
        for j in range(NY):
            cc, rows = chunk_of(h, j)
            if j < NY - 1:
                send_out(0, h, cc, False)
            else:
                send_out(0, h, cc, True)

    weights_first()
    for which in ((6,), (0, 1, 2, 3), (4, 5)):
        for a in (0, 1):
            for h in (0, 1):
                send_in(a, h, which)
    weights_second()
    for cp in wcp:
        cp.wait()
    for off in (0, 1, 3):
        key_forward(0, off)
    weights_third()
    for off in (0, 1, 3):
        key_forward(1, off)
    key_forward(0, 2)
    for m in range(3):
        rs_x_start(0, 0, m)
    send_in(2, 1)
    send_in(3, 1)
    key_forward(1, 2)
    for m in range(3):
        rs_x_start(0, 1, m)
    send_in(2, 0)
    send_in(3, 0)
    for step in (rs_x_finish, rs_z_finish, ag_z_finish):
        for h in range(2):
            for m in range(3):
                step(0, h, m)
    for h in range(2):
        for m in range(3):
            ag_x_finish(0, h, m)
        for off in range(NY):
            wait_in(2, h, off)
            wait_in(3, h, off)
        query_side(h)
        for m in range(3):
            rs_x_start(1, h, m)
    for h in range(2):
        send_query(h)
    for step in (rs_x_finish, rs_z_finish, ag_z_finish, ag_x_finish):
        for h in range(2):
            for m in range(3):
                step(1, h, m)
    key_back()

    @pl.when(diagonal)
    def _():
        wait_bytes(wz.at[pl.ds(0, 3)], w1s)

    wait_bytes(wz.at[pl.ds(0, NZ - 1)], w2s)
    wait_bytes(lq.at[pl.ds(0, 3)], l1s)
    wait_bytes(lq.at[pl.ds(0, 3)], l2s)
    for h in range(2):
        for a in range(4):
            wait_bytes(buf.at[a, h, pl.ds(0, ALL - ROWS)], in_send.at[a, h])
        for f in range(2):
            for m in range(3):
                wait_bytes(rx.at[f, h, m], xs.at[f, h, m])
                wait_bytes(rz.at[f, h, m], zsd.at[f, h, m])
                wait_bytes(rz.at[f, h, m], azs.at[f, h, m])
                wait_bytes(rx.at[f, h, m], axs.at[f, h, m])
        for a in range(3):
            wait_bytes(stage.at[a, h, pl.ds(0, ALL - ROWS)], out_send.at[a, h])
            wait_bytes(stage.at[a, h, pl.ds(0, ALL - ROWS)], out_recv.at[a, h])
            wait_bytes(stage.at[a, h, pl.ds(0, ROWS)], out_loc.at[a, h])


def body(queries, key_tokens, values, out_grad, learn_rates, w_gate, w_up, w_down):
    scale = 1.0 / math.sqrt(DH * ALL * NX * NZ)
    dma = pltpu.SemaphoreType.DMA
    out = jax.ShapeDtypeStruct(queries.shape, BF16)
    return pl.pallas_call(
        functools.partial(kernel, scale),
        out_shape=(out, out, out),
        in_specs=[pl.BlockSpec(memory_space=pl.ANY)] * 8,
        out_specs=[pl.BlockSpec(memory_space=pl.ANY)] * 3,
        scratch_shapes=[
            pltpu.VMEM((4, 2, ALL, DH), BF16),
            pltpu.VMEM((2, ALL, 128), F32),
            pltpu.VMEM((2, ALL), F32),
            pltpu.VMEM((NY, 8, CHUNK), F32),
            pltpu.VMEM((NY, 8, CHUNK), F32),
            pltpu.VMEM((NX, 8, CHUNK), F32),
            pltpu.VMEM((NZ, 3, EIGHTH, DH), BF16),
            pltpu.VMEM((2, 3 * DH, DH), BF16),
            pltpu.VMEM((2, 2, 3 * DH, DH), F32),
            pltpu.VMEM((2, 2, 3 * DH, DH), BF16),
            pltpu.VMEM((2, 2, 3, NX - 1, PART, DH), BF16),
            pltpu.VMEM((2, 2, 3, PART, DH), F32),
            pltpu.VMEM((2, 2, 3, PART, DH), BF16),
            pltpu.VMEM((2, 2, 3, NZ - 1, ZROWS, ZCOLS), BF16),
            pltpu.VMEM((2, 2, 3 * DH, DH), BF16),
            pltpu.VMEM((2, ALL, DH), F32),
            pltpu.VMEM((2, ALL, DH), F32),
            pltpu.VMEM((2, ALL, DH), F32),
            pltpu.VMEM((2, ALL, DH), BF16),
            pltpu.VMEM((2, ALL, DH), BF16),
            pltpu.VMEM((2, ALL, DH), BF16),
            pltpu.VMEM((2, ALL, DH), BF16),
            pltpu.VMEM((3, 2, ALL, DH), BF16),
            dma((4, 2)), dma((4, 2, NY)), dma((4, 2)), dma((2, 3)), dma,
            dma, dma, dma, dma, dma, dma, dma, dma,
            dma((2, 2, 3)), dma((2, 2, 3)), dma((2, 2, 3)), dma((2, 2, 3)),
            dma((2, 2, 3)), dma((2, 2, 3)), dma((2, 2, 3)), dma((2, 2, 3)),
            dma((3, 2)), dma((3, 2)), dma((3, 2)),
        ],
        compiler_params=pltpu.CompilerParams(
            collective_id=0, has_side_effects=True, vmem_limit_bytes=60 << 20
        ),
    )(queries, key_tokens, values, out_grad, learn_rates.T, w_gate, w_up, w_down)


def solution(mesh):
    tokens = P(("tok", "head"), None)
    heads = P("head", None, None)
    return jax.shard_map(
        body,
        mesh=mesh,
        in_specs=(tokens, tokens, tokens, tokens, P("tok", "head"), heads, heads, heads),
        out_specs=(tokens, tokens, tokens),
        check_vma=False,
    )
```

```python
import functools
import math

import jax
import jax.numpy as jnp
from jax import lax
from jax.experimental import pallas as pl
from jax.experimental.pallas import tpu as pltpu
from jax.sharding import PartitionSpec as P

DH = 256
NX, NZ, NY, NC = 4, 8, 4, 2
NH = NY * NC
ROWS = 128
ALL = NH * ROWS
PART = DH // NX
ZROWS, ZCOLS = 16, 128
EIGHTH = DH // NZ
CHUNK = 256
MESH = pl.DeviceIdType.MESH
F32 = jnp.float32
BF16 = jnp.bfloat16


def mm(a, b):
    return jnp.dot(a, b, preferred_element_type=F32)


def mm_rt(a, b):
    return lax.dot_general(a, b, (((1,), (1,)), ((), ())), preferred_element_type=F32)


def mm_lt(a, b):
    return lax.dot_general(a, b, (((0,), (0,)), ((), ())), preferred_element_type=F32)


def kernel(
    scale,
    q_in, k_in, v_in, o_in, lr_in, wg_in, wu_in, wd_in,
    gq_out, gk_out, gv_out,
    buf, lrc, lrow, lsend, lq, lfin, wz, w, acc, pb, rx, zf, zs, rz, full,
    gate, upper, dhid, hid, dgate, dup, scaled, stage,
    in_send, in_recv, in_loc, w_sem, lr_sem, w1s, w1r, w2s, w2r, l1s, l1r, l2s, l2r,
    xs, xr, zsd, zrv, azs, azr, axs, axr,
    out_send, out_recv, out_loc,
):
    tok, me = lax.axis_index("tok"), lax.axis_index("head")
    x, z = tok // NZ, tok % NZ
    y, c = me // NC, me % NC
    ins = (k_in, v_in, q_in, o_in)
    outs = (gq_out, gk_out, gv_out)

    spots = [(1, 0), (3, 0), (1, 1), (3, 1), (2, 0), (2, 1), (0, 1)]
    chip = (y, x)
    line = (me, x * NC + c)
    lpeers = [
        [(lax.rem(chip[g] + dp, NY) * NC + lax.rem(c + dc, NC)) for dp, dc in spots] for g in range(2)
    ]
    cpos = (x, y)
    cpeers = [[lax.rem(cpos[g] + d, NX) for d in (2, 1, 3)] for g in range(2)]
    zpeers = [lax.rem(z + d, NZ) for d in (4, 3, 5, 2, 6, 1, 7)]

    def ldev(g, p):
        return (tok, p) if g == 0 else ((p // NC) * NZ + z, y * NC + p % NC)

    def cdev(g, p):
        return (p * NZ + z, me) if g == 0 else (tok, p * NC + c)

    def zdev(pz):
        return (x * NZ + pz, me)

    barrier = pltpu.get_barrier_semaphore()
    greet = [ldev(0, p) for p in lpeers[0]] + [ldev(1, p) for p in lpeers[1][:-1]] + [zdev(p) for p in zpeers]
    for p in greet:
        pl.semaphore_signal(barrier, inc=1, device_id=p, device_id_type=MESH)

    def cols(p, h):
        return pl.ds(pl.multiple_of(p * (2 * DH) + h * DH, DH), DH)

    def rows_of(p):
        return pl.ds(pl.multiple_of(p * ROWS, ROWS), ROWS)

    def local_in(a, h):
        cp = pltpu.make_async_copy(ins[a].at[:, cols(line[h], h)], buf.at[a, h, rows_of(line[h])], in_loc.at[a, h])
        cp.start()
        return cp

    w_in = (wg_in, wu_in, wd_in)
    eighth = pl.ds(pl.multiple_of(z * EIGHTH, EIGHTH), EIGHTH)
    diagonal = x == y
    wcp = []
    for m in range(3):
        wcp.append(pltpu.make_async_copy(w_in[m].at[0], w.at[0, pl.ds(m * DH, DH)], w_sem.at[0, m]))
    lcp = pltpu.make_async_copy(lr_in, lrow, lr_sem)
    lcp.start()
    for cp in wcp:
        cp.start()
    locals_in = {(a, h): local_in(a, h) for h in range(2) for a in range(4)}
    lcp.wait()
    for i in range(NY):
        lsend[i] = jnp.broadcast_to(lrow[1:2, i * CHUNK:(i + 1) * CHUNK], (8, CHUNK))
    lq[y] = lsend[y]

    pl.semaphore_wait(barrier, len(greet))

    def column(row):
        return jnp.broadcast_to(row, (128, CHUNK)).T

    def weights_first():
        @pl.when(diagonal)
        def _():
            for m in range(3):
                pltpu.make_async_copy(w_in[m].at[1, eighth], wz.at[z, m], w_sem.at[1, m]).start()
                for p in cpeers[1]:
                    pltpu.make_async_remote_copy(
                        src_ref=w_in[m].at[1, eighth],
                        dst_ref=wz.at[z, m],
                        send_sem=w1s,
                        recv_sem=w1r,
                        device_id=cdev(1, p),
                        device_id_type=MESH,
                    ).start()

        for p in cpeers[1]:
            pltpu.make_async_remote_copy(
                src_ref=lsend.at[p],
                dst_ref=lq.at[y],
                send_sem=l1s,
                recv_sem=l1r,
                device_id=cdev(1, p),
                device_id_type=MESH,
            ).start()

    def weights_second():
        @pl.when(diagonal)
        def _():
            for m in range(3):
                wait_bytes(wz.at[0, m], w_sem.at[1, m])

        @pl.when(jnp.logical_not(diagonal))
        def _():
            wait_bytes(wz.at[0], w1r)

        for p in zpeers:
            pltpu.make_async_remote_copy(
                src_ref=wz.at[z],
                dst_ref=wz.at[z],
                send_sem=w2s,
                recv_sem=w2r,
                device_id=zdev(p),
                device_id_type=MESH,
            ).start()
        wait_bytes(lq.at[pl.ds(0, 3)], l1r)
        for p in cpeers[0]:
            pltpu.make_async_remote_copy(
                src_ref=lq.at[p],
                dst_ref=lfin.at[x],
                send_sem=l2s,
                recv_sem=l2r,
                device_id=cdev(0, p),
                device_id_type=MESH,
            ).start()
        lfin[x] = lq[x]
        for i in range(NY):
            lrc[0, pl.ds(i * CHUNK, CHUNK)] = column(lrow[0:1, i * CHUNK:(i + 1) * CHUNK])

    def weights_third():
        wait_bytes(wz.at[pl.ds(0, NZ - 1)], w2r)
        wait_bytes(lq.at[pl.ds(0, 3)], l2r)
        for i in range(NZ):
            for m in range(3):
                w[1, pl.ds(m * DH + i * EIGHTH, EIGHTH)] = wz[i, m]
        for i in range(NX):
            lrc[1, pl.ds(i * CHUNK, CHUNK)] = column(lfin[i, 0:1])

    def rates(h, rows):
        col = lrc[h, rows]
        return jnp.concatenate([col, col], axis=1)

    def send_in(a, h, which=range(7)):
        for p in [lpeers[h][i] for i in which]:
            pltpu.make_async_remote_copy(
                src_ref=ins[a].at[:, cols(p, h)],
                dst_ref=buf.at[a, h, rows_of(line[h])],
                send_sem=in_send.at[a, h],
                recv_sem=in_recv.at[a, h, chip[h]],
                device_id=ldev(h, p),
                device_id_type=MESH,
            ).start()

    def wait_bytes(ref, sem):
        pltpu.make_async_copy(ref, ref, sem).wait()

    def wait_in(a, h, off):
        cc = lax.rem(chip[h] + off, NY)
        if off == 0:
            locals_in[(a, h)].wait()
            wait_bytes(buf.at[a, h, pl.ds(0, ROWS)], in_recv.at[a, h, cc])
        else:
            wait_bytes(buf.at[a, h, pl.ds(0, CHUNK)], in_recv.at[a, h, cc])

    def silu_parts(gp):
        s = 0.5 * jnp.tanh(0.5 * gp) + 0.5
        act = gp * s
        rest = 1.0 - s
        return s, act, rest, s + act * rest

    def key_forward(h, off):
        wait_in(0, h, off)
        wait_in(1, h, off)
        cc = lax.rem(chip[h] + off, NY)
        rows = pl.ds(pl.multiple_of(cc * CHUNK, CHUNK), CHUNK)
        kr = buf[0, h, rows]
        sc = (rates(h, rows) * buf[1, h, rows].astype(F32)).astype(BF16)
        scaled[h, rows] = sc
        gp = mm(kr, w[h, 0:DH])
        up = mm(kr, w[h, DH:2 * DH])
        kd = mm_rt(sc, w[h, 2 * DH:3 * DH])
        s, act, rest, slope = silu_parts(gp)
        hd = (act * up).astype(BF16)
        dg = (kd * up * slope).astype(BF16)
        du = (kd * act).astype(BF16)
        gate[h, rows] = gp
        upper[h, rows] = up
        dhid[h, rows] = kd
        hid[h, rows] = hd
        dgate[h, rows] = dg
        dup[h, rows] = du
        for m, term in enumerate((mm_lt(kr, dg), mm_lt(kr, du), mm_lt(hd, sc))):
            mat = pl.ds(m * DH, DH)
            acc[0, h, mat] = term if off == 0 else acc[0, h, mat] + term

    def part(m, p):
        return pl.ds(pl.multiple_of(m * DH + p * PART, PART), PART)

    def zrow(p):
        return pl.multiple_of((p // 2) * ZROWS, ZROWS)

    def zcol(p):
        return pl.ds(pl.multiple_of((p % 2) * ZCOLS, ZCOLS), ZCOLS)

    def rs_x_start(f, h, m):
        mat = pl.ds(m * DH, DH)
        pb[f, h, mat] = acc[f, h, mat].astype(BF16)
        for i, p in enumerate(cpeers[h]):
            pltpu.make_async_remote_copy(
                src_ref=pb.at[f, h, part(m, p)],
                dst_ref=rx.at[f, h, m, i],
                send_sem=xs.at[f, h, m],
                recv_sem=xr.at[f, h, m],
                device_id=cdev(h, p),
                device_id_type=MESH,
            ).start()

    def rs_x_finish(f, h, m):
        wait_bytes(rx.at[f, h, m], xr.at[f, h, m])
        total = acc[f, h, part(m, cpos[h])]
        for i in range(NX - 1):
            total = total + rx[f, h, m, i].astype(F32)
        zf[f, h, m] = total
        zs[f, h, m] = total.astype(BF16)
        for i, p in enumerate(zpeers):
            pltpu.make_async_remote_copy(
                src_ref=zs.at[f, h, m, pl.ds(zrow(p), ZROWS), zcol(p)],
                dst_ref=rz.at[f, h, m, i],
                send_sem=zsd.at[f, h, m],
                recv_sem=zrv.at[f, h, m],
                device_id=zdev(p),
                device_id_type=MESH,
            ).start()

    def rs_z_finish(f, h, m):
        wait_bytes(rz.at[f, h, m], zrv.at[f, h, m])
        total = zf[f, h, m, pl.ds(zrow(z), ZROWS), zcol(z)]
        for i in range(NZ - 1):
            total = total + rz[f, h, m, i].astype(F32)
        own = pl.ds(pl.multiple_of(m * DH + cpos[h] * PART + zrow(z), ZROWS), ZROWS)
        total = total * scale
        if f == 0:
            total = w[h, own, zcol(z)].astype(F32) + total
        full[f, h, own, zcol(z)] = total.astype(BF16)
        for p in zpeers:
            pltpu.make_async_remote_copy(
                src_ref=full.at[f, h, own, zcol(z)],
                dst_ref=full.at[f, h, own, zcol(z)],
                send_sem=azs.at[f, h, m],
                recv_sem=azr.at[f, h, m],
                device_id=zdev(p),
                device_id_type=MESH,
            ).start()

    def ag_z_finish(f, h, m):
        wait_bytes(rz.at[f, h, m], azr.at[f, h, m])
        for p in cpeers[h]:
            pltpu.make_async_remote_copy(
                src_ref=full.at[f, h, part(m, cpos[h])],
                dst_ref=full.at[f, h, part(m, cpos[h])],
                send_sem=axs.at[f, h, m],
                recv_sem=axr.at[f, h, m],
                device_id=cdev(h, p),
                device_id_type=MESH,
            ).start()

    def ag_x_finish(f, h, m):
        wait_bytes(rx.at[f, h, m], axr.at[f, h, m])

    def send_out(a, h, cc, own_chip):
        def remote(p):
            pltpu.make_async_remote_copy(
                src_ref=stage.at[a, h, rows_of(p)],
                dst_ref=outs[a].at[:, cols(line[h], h)],
                send_sem=out_send.at[a, h],
                recv_sem=out_recv.at[a, h],
                device_id=ldev(h, p),
                device_id_type=MESH,
            ).start()

        @pl.when(jnp.logical_not(own_chip))
        def _():
            for core in range(NC):
                remote(cc * NC + core)

        @pl.when(own_chip)
        def _():
            remote(chip[h] * NC + (1 - c))
            pltpu.make_async_copy(
                stage.at[a, h, rows_of(line[h])], outs[a].at[:, cols(line[h], h)], out_loc.at[a, h]
            ).start()

    def chunk_of(h, j):
        cc = lax.rem(chip[h] + 2 + j + j // 2 + 2 * (j // 3), NY)
        return cc, pl.ds(pl.multiple_of(cc * CHUNK, CHUNK), CHUNK)

    def query_side(h):
        qr = buf[2, h]
        orr = buf[3, h]
        ng = full[0, h, 0:DH]
        nu = full[0, h, DH:2 * DH]
        gp = mm(qr, ng)
        up = mm(qr, nu)
        qd = mm_rt(orr, full[0, h, 2 * DH:3 * DH])
        s, act, rest, slope = silu_parts(gp)
        hd = (act * up).astype(BF16)
        dg = (qd * up * slope).astype(BF16)
        du = (qd * act).astype(BF16)
        acc[1, h, 0:DH] = mm_lt(qr, dg)
        acc[1, h, DH:2 * DH] = mm_lt(qr, du)
        acc[1, h, 2 * DH:3 * DH] = mm_lt(hd, orr)
        stage[0, h] = (mm_rt(dg, ng) + mm_rt(du, nu)).astype(BF16)

    def back(h, j):
        yy, rows = chunk_of(h, j)
        kr = buf[0, h, rows]
        ag = full[1, h, 0:DH]
        au = full[1, h, DH:2 * DH]
        ad = full[1, h, 2 * DH:3 * DH]
        bdg = mm(kr, ag)
        bdu = mm(kr, au)
        bh = mm_rt(scaled[h, rows], ad)
        gp = gate[h, rows]
        up = upper[h, rows]
        kd = dhid[h, rows]
        s, act, rest, slope = silu_parts(gp)
        twice = s + s
        curve = rest * (twice + act * (1.0 - twice))
        bdh = (bdg * up * slope + bdu * act).astype(BF16)
        bg = (bdg * kd * up * curve + (bdu * kd + bh * up) * slope).astype(BF16)
        bu = (bdg * kd * slope + bh * act).astype(BF16)
        kg = mm_rt(dgate[h, rows], ag) + mm_rt(dup[h, rows], au)
        kg = kg + mm_rt(bg, w[h, 0:DH]) + mm_rt(bu, w[h, DH:2 * DH])
        stage[1, h, rows] = kg.astype(BF16)
        vg = mm(hid[h, rows], ad) + mm(bdh, w[h, 2 * DH:3 * DH])
        stage[2, h, rows] = (rates(h, rows) * vg).astype(BF16)
        return yy

    def key_back():
        def step(j, carry):
            spots_of = (back(0, j), back(1, j))
            for a in (1, 2):
                for h in range(2):
                    send_out(a, h, spots_of[h], j == NY - 1)
            return carry

        lax.fori_loop(0, NY, step, 0)

    def send_query(h):
        for j in range(NY):
            cc, rows = chunk_of(h, j)
            if j < NY - 1:
                send_out(0, h, cc, False)
            else:
                send_out(0, h, cc, True)

    weights_first()
    for which in ((6,), (0, 1, 2, 3), (4, 5)):
        for a in (0, 1):
            for h in (0, 1):
                send_in(a, h, which)
    weights_second()
    for cp in wcp:
        cp.wait()
    for off in (0, 1, 3):
        key_forward(0, off)
    weights_third()
    for off in (0, 1, 3):
        key_forward(1, off)
    key_forward(0, 2)
    for m in range(3):
        rs_x_start(0, 0, m)
    send_in(2, 1)
    send_in(3, 1)
    key_forward(1, 2)
    for m in range(3):
        rs_x_start(0, 1, m)
    send_in(2, 0)
    send_in(3, 0)
    for step in (rs_x_finish, rs_z_finish, ag_z_finish):
        for h in range(2):
            for m in range(3):
                step(0, h, m)
    for h in range(2):
        for m in range(3):
            ag_x_finish(0, h, m)
        for off in range(NY):
            wait_in(2, h, off)
            wait_in(3, h, off)
        query_side(h)
        for m in range(3):
            rs_x_start(1, h, m)
    for h in range(2):
        send_query(h)
    for step in (rs_x_finish, rs_z_finish, ag_z_finish, ag_x_finish):
        for h in range(2):
            for m in range(3):
                step(1, h, m)
    key_back()

    @pl.when(diagonal)
    def _():
        wait_bytes(wz.at[pl.ds(0, 3)], w1s)

    wait_bytes(wz.at[pl.ds(0, NZ - 1)], w2s)
    wait_bytes(lq.at[pl.ds(0, 3)], l1s)
    wait_bytes(lq.at[pl.ds(0, 3)], l2s)
    for h in range(2):
        for a in range(4):
            wait_bytes(buf.at[a, h, pl.ds(0, ALL - ROWS)], in_send.at[a, h])
        for f in range(2):
            for m in range(3):
                wait_bytes(rx.at[f, h, m], xs.at[f, h, m])
                wait_bytes(rz.at[f, h, m], zsd.at[f, h, m])
                wait_bytes(rz.at[f, h, m], azs.at[f, h, m])
                wait_bytes(rx.at[f, h, m], axs.at[f, h, m])
        for a in range(3):
            wait_bytes(stage.at[a, h, pl.ds(0, ALL - ROWS)], out_send.at[a, h])
            wait_bytes(stage.at[a, h, pl.ds(0, ALL - ROWS)], out_recv.at[a, h])
            wait_bytes(stage.at[a, h, pl.ds(0, ROWS)], out_loc.at[a, h])


def body(queries, key_tokens, values, out_grad, learn_rates, w_gate, w_up, w_down):
    scale = 1.0 / math.sqrt(DH * ALL * NX * NZ)
    dma = pltpu.SemaphoreType.DMA
    out = jax.ShapeDtypeStruct(queries.shape, BF16)
    return pl.pallas_call(
        functools.partial(kernel, scale),
        out_shape=(out, out, out),
        in_specs=[pl.BlockSpec(memory_space=pl.ANY)] * 8,
        out_specs=[pl.BlockSpec(memory_space=pl.ANY)] * 3,
        scratch_shapes=[
            pltpu.VMEM((4, 2, ALL, DH), BF16),
            pltpu.VMEM((2, ALL, 128), F32),
            pltpu.VMEM((2, ALL), F32),
            pltpu.VMEM((NY, 8, CHUNK), F32),
            pltpu.VMEM((NY, 8, CHUNK), F32),
            pltpu.VMEM((NX, 8, CHUNK), F32),
            pltpu.VMEM((NZ, 3, EIGHTH, DH), BF16),
            pltpu.VMEM((2, 3 * DH, DH), BF16),
            pltpu.VMEM((2, 2, 3 * DH, DH), F32),
            pltpu.VMEM((2, 2, 3 * DH, DH), BF16),
            pltpu.VMEM((2, 2, 3, NX - 1, PART, DH), BF16),
            pltpu.VMEM((2, 2, 3, PART, DH), F32),
            pltpu.VMEM((2, 2, 3, PART, DH), BF16),
            pltpu.VMEM((2, 2, 3, NZ - 1, ZROWS, ZCOLS), BF16),
            pltpu.VMEM((2, 2, 3 * DH, DH), BF16),
            pltpu.VMEM((2, ALL, DH), F32),
            pltpu.VMEM((2, ALL, DH), F32),
            pltpu.VMEM((2, ALL, DH), F32),
            pltpu.VMEM((2, ALL, DH), BF16),
            pltpu.VMEM((2, ALL, DH), BF16),
            pltpu.VMEM((2, ALL, DH), BF16),
            pltpu.VMEM((2, ALL, DH), BF16),
            pltpu.VMEM((3, 2, ALL, DH), BF16),
            dma((4, 2)), dma((4, 2, NY)), dma((4, 2)), dma((2, 3)), dma,
            dma, dma, dma, dma, dma, dma, dma, dma,
            dma((2, 2, 3)), dma((2, 2, 3)), dma((2, 2, 3)), dma((2, 2, 3)),
            dma((2, 2, 3)), dma((2, 2, 3)), dma((2, 2, 3)), dma((2, 2, 3)),
            dma((3, 2)), dma((3, 2)), dma((3, 2)),
        ],
        compiler_params=pltpu.CompilerParams(
            collective_id=0, has_side_effects=True, vmem_limit_bytes=60 << 20
        ),
    )(queries, key_tokens, values, out_grad, learn_rates.T, w_gate, w_up, w_down)


def solution(mesh):
    tokens = P(("tok", "head"), None)
    heads = P("head", None, None)
    return jax.shard_map(
        body,
        mesh=mesh,
        in_specs=(tokens, tokens, tokens, tokens, P("tok", "head"), heads, heads, heads),
        out_specs=(tokens, tokens, tokens),
        check_vma=False,
    )
```

```python
import functools
import math

import jax
import jax.numpy as jnp
from jax import lax
from jax.experimental import pallas as pl
from jax.experimental.pallas import tpu as pltpu
from jax.sharding import PartitionSpec as P

DH = 256
NX, NZ, NY, NC = 4, 8, 4, 2
NH = NY * NC
ROWS = 128
ALL = NH * ROWS
PART = DH // NX
ZROWS, ZCOLS = 16, 128
EIGHTH = DH // NZ
CHUNK = 256
MESH = pl.DeviceIdType.MESH
F32 = jnp.float32
BF16 = jnp.bfloat16


def mm(a, b):
    return jnp.dot(a, b, preferred_element_type=F32)


def mm_rt(a, b):
    return lax.dot_general(a, b, (((1,), (1,)), ((), ())), preferred_element_type=F32)


def mm_lt(a, b):
    return lax.dot_general(a, b, (((0,), (0,)), ((), ())), preferred_element_type=F32)


def kernel(
    scale,
    q_in, k_in, v_in, o_in, lr_in, wg_in, wu_in, wd_in,
    gq_out, gk_out, gv_out,
    buf, lrc, lrow, lsend, lq, lfin, wz, w, acc, pb, rx, zf, zs, rz, full,
    gate, upper, dhid, hid, dgate, dup, scaled, stage,
    in_send, in_recv, in_loc, w_sem, lr_sem, w1s, w1r, w2s, w2r, l1s, l1r, l2s, l2r,
    xs, xr, zsd, zrv, azs, azr, axs, axr,
    out_send, out_recv, out_loc,
):
    tok, me = lax.axis_index("tok"), lax.axis_index("head")
    x, z = tok // NZ, tok % NZ
    y, c = me // NC, me % NC
    ins = (k_in, v_in, q_in, o_in)
    outs = (gq_out, gk_out, gv_out)

    spots = [(1, 0), (3, 0), (1, 1), (3, 1), (2, 0), (2, 1), (0, 1)]
    chip = (y, x)
    line = (me, x * NC + c)
    lpeers = [
        [(lax.rem(chip[g] + dp, NY) * NC + lax.rem(c + dc, NC)) for dp, dc in spots] for g in range(2)
    ]
    cpos = (x, y)
    cpeers = [[lax.rem(cpos[g] + d, NX) for d in (2, 1, 3)] for g in range(2)]
    zpeers = [lax.rem(z + d, NZ) for d in (4, 3, 5, 2, 6, 1, 7)]

    def ldev(g, p):
        return (tok, p) if g == 0 else ((p // NC) * NZ + z, y * NC + p % NC)

    def cdev(g, p):
        return (p * NZ + z, me) if g == 0 else (tok, p * NC + c)

    def zdev(pz):
        return (x * NZ + pz, me)

    barrier = pltpu.get_barrier_semaphore()
    greet = [ldev(0, p) for p in lpeers[0]] + [ldev(1, p) for p in lpeers[1][:-1]] + [zdev(p) for p in zpeers]
    for p in greet:
        pl.semaphore_signal(barrier, inc=1, device_id=p, device_id_type=MESH)

    def cols(p, h):
        return pl.ds(pl.multiple_of(p * (2 * DH) + h * DH, DH), DH)

    def rows_of(p):
        return pl.ds(pl.multiple_of(p * ROWS, ROWS), ROWS)

    def local_in(a, h):
        cp = pltpu.make_async_copy(ins[a].at[:, cols(line[h], h)], buf.at[a, h, rows_of(line[h])], in_loc.at[a, h])
        cp.start()
        return cp

    w_in = (wg_in, wu_in, wd_in)
    eighth = pl.ds(pl.multiple_of(z * EIGHTH, EIGHTH), EIGHTH)
    diagonal = x == y
    wcp = []
    for m in range(3):
        wcp.append(pltpu.make_async_copy(w_in[m].at[0], w.at[0, pl.ds(m * DH, DH)], w_sem.at[0, m]))
    lcp = pltpu.make_async_copy(lr_in, lrow, lr_sem)
    lcp.start()
    for cp in wcp:
        cp.start()
    locals_in = {(a, h): local_in(a, h) for h in range(2) for a in range(4)}
    lcp.wait()
    for i in range(NY):
        lsend[i] = jnp.broadcast_to(lrow[1:2, i * CHUNK:(i + 1) * CHUNK], (8, CHUNK))
    lq[y] = lsend[y]

    pl.semaphore_wait(barrier, len(greet))

    def column(row):
        return jnp.broadcast_to(row, (128, CHUNK)).T

    def weights_first():
        @pl.when(diagonal)
        def _():
            for m in range(3):
                pltpu.make_async_copy(w_in[m].at[1, eighth], wz.at[z, m], w_sem.at[1, m]).start()
                for p in cpeers[1]:
                    pltpu.make_async_remote_copy(
                        src_ref=w_in[m].at[1, eighth],
                        dst_ref=wz.at[z, m],
                        send_sem=w1s,
                        recv_sem=w1r,
                        device_id=cdev(1, p),
                        device_id_type=MESH,
                    ).start()

        for p in cpeers[1]:
            pltpu.make_async_remote_copy(
                src_ref=lsend.at[p],
                dst_ref=lq.at[y],
                send_sem=l1s,
                recv_sem=l1r,
                device_id=cdev(1, p),
                device_id_type=MESH,
            ).start()

    def weights_second():
        @pl.when(diagonal)
        def _():
            for m in range(3):
                wait_bytes(wz.at[0, m], w_sem.at[1, m])

        @pl.when(jnp.logical_not(diagonal))
        def _():
            wait_bytes(wz.at[0], w1r)

        for p in zpeers:
            pltpu.make_async_remote_copy(
                src_ref=wz.at[z],
                dst_ref=wz.at[z],
                send_sem=w2s,
                recv_sem=w2r,
                device_id=zdev(p),
                device_id_type=MESH,
            ).start()
        wait_bytes(lq.at[pl.ds(0, 3)], l1r)
        for p in cpeers[0]:
            pltpu.make_async_remote_copy(
                src_ref=lq.at[p],
                dst_ref=lfin.at[x],
                send_sem=l2s,
                recv_sem=l2r,
                device_id=cdev(0, p),
                device_id_type=MESH,
            ).start()
        lfin[x] = lq[x]
        for i in range(NY):
            lrc[0, pl.ds(i * CHUNK, CHUNK)] = column(lrow[0:1, i * CHUNK:(i + 1) * CHUNK])

    def weights_third():
        wait_bytes(wz.at[pl.ds(0, NZ - 1)], w2r)
        wait_bytes(lq.at[pl.ds(0, 3)], l2r)
        for i in range(NZ):
            for m in range(3):
                w[1, pl.ds(m * DH + i * EIGHTH, EIGHTH)] = wz[i, m]
        for i in range(NX):
            lrc[1, pl.ds(i * CHUNK, CHUNK)] = column(lfin[i, 0:1])

    def rates(h, rows):
        col = lrc[h, rows]
        return jnp.concatenate([col, col], axis=1)

    def send_in(a, h, which=range(7)):
        for p in [lpeers[h][i] for i in which]:
            pltpu.make_async_remote_copy(
                src_ref=ins[a].at[:, cols(p, h)],
                dst_ref=buf.at[a, h, rows_of(line[h])],
                send_sem=in_send.at[a, h],
                recv_sem=in_recv.at[a, h, chip[h]],
                device_id=ldev(h, p),
                device_id_type=MESH,
            ).start()

    def wait_bytes(ref, sem):
        pltpu.make_async_copy(ref, ref, sem).wait()

    def wait_in(a, h, off):
        cc = lax.rem(chip[h] + off, NY)
        if off == 0:
            locals_in[(a, h)].wait()
            wait_bytes(buf.at[a, h, pl.ds(0, ROWS)], in_recv.at[a, h, cc])
        else:
            wait_bytes(buf.at[a, h, pl.ds(0, CHUNK)], in_recv.at[a, h, cc])

    def silu_parts(gp):
        s = 0.5 * jnp.tanh(0.5 * gp) + 0.5
        act = gp * s
        rest = 1.0 - s
        return s, act, rest, s + act * rest

    def key_forward(h, off):
        wait_in(0, h, off)
        wait_in(1, h, off)
        cc = lax.rem(chip[h] + off, NY)
        rows = pl.ds(pl.multiple_of(cc * CHUNK, CHUNK), CHUNK)
        kr = buf[0, h, rows]
        sc = (rates(h, rows) * buf[1, h, rows].astype(F32)).astype(BF16)
        scaled[h, rows] = sc
        gp = mm(kr, w[h, 0:DH])
        up = mm(kr, w[h, DH:2 * DH])
        kd = mm_rt(sc, w[h, 2 * DH:3 * DH])
        s, act, rest, slope = silu_parts(gp)
        hd = (act * up).astype(BF16)
        dg = (kd * up * slope).astype(BF16)
        du = (kd * act).astype(BF16)
        gate[h, rows] = gp
        upper[h, rows] = up
        dhid[h, rows] = kd
        hid[h, rows] = hd
        dgate[h, rows] = dg
        dup[h, rows] = du
        for m, term in enumerate((mm_lt(kr, dg), mm_lt(kr, du), mm_lt(hd, sc))):
            mat = pl.ds(m * DH, DH)
            acc[0, h, mat] = term if off == 0 else acc[0, h, mat] + term

    def part(m, p):
        return pl.ds(pl.multiple_of(m * DH + p * PART, PART), PART)

    def zrow(p):
        return pl.multiple_of((p // 2) * ZROWS, ZROWS)

    def zcol(p):
        return pl.ds(pl.multiple_of((p % 2) * ZCOLS, ZCOLS), ZCOLS)

    def rs_x_start(f, h, m):
        mat = pl.ds(m * DH, DH)
        pb[f, h, mat] = acc[f, h, mat].astype(BF16)
        for i, p in enumerate(cpeers[h]):
            pltpu.make_async_remote_copy(
                src_ref=pb.at[f, h, part(m, p)],
                dst_ref=rx.at[f, h, m, i],
                send_sem=xs.at[f, h, m],
                recv_sem=xr.at[f, h, m],
                device_id=cdev(h, p),
                device_id_type=MESH,
            ).start()

    def rs_x_finish(f, h, m):
        wait_bytes(rx.at[f, h, m], xr.at[f, h, m])
        total = acc[f, h, part(m, cpos[h])]
        for i in range(NX - 1):
            total = total + rx[f, h, m, i].astype(F32)
        zf[f, h, m] = total
        zs[f, h, m] = total.astype(BF16)
        for i, p in enumerate(zpeers):
            pltpu.make_async_remote_copy(
                src_ref=zs.at[f, h, m, pl.ds(zrow(p), ZROWS), zcol(p)],
                dst_ref=rz.at[f, h, m, i],
                send_sem=zsd.at[f, h, m],
                recv_sem=zrv.at[f, h, m],
                device_id=zdev(p),
                device_id_type=MESH,
            ).start()

    def rs_z_finish(f, h, m):
        wait_bytes(rz.at[f, h, m], zrv.at[f, h, m])
        total = zf[f, h, m, pl.ds(zrow(z), ZROWS), zcol(z)]
        for i in range(NZ - 1):
            total = total + rz[f, h, m, i].astype(F32)
        own = pl.ds(pl.multiple_of(m * DH + cpos[h] * PART + zrow(z), ZROWS), ZROWS)
        total = total * scale
        if f == 0:
            total = w[h, own, zcol(z)].astype(F32) + total
        full[f, h, own, zcol(z)] = total.astype(BF16)
        for p in zpeers:
            pltpu.make_async_remote_copy(
                src_ref=full.at[f, h, own, zcol(z)],
                dst_ref=full.at[f, h, own, zcol(z)],
                send_sem=azs.at[f, h, m],
                recv_sem=azr.at[f, h, m],
                device_id=zdev(p),
                device_id_type=MESH,
            ).start()

    def ag_z_finish(f, h, m):
        wait_bytes(rz.at[f, h, m], azr.at[f, h, m])
        for p in cpeers[h]:
            pltpu.make_async_remote_copy(
                src_ref=full.at[f, h, part(m, cpos[h])],
                dst_ref=full.at[f, h, part(m, cpos[h])],
                send_sem=axs.at[f, h, m],
                recv_sem=axr.at[f, h, m],
                device_id=cdev(h, p),
                device_id_type=MESH,
            ).start()

    def ag_x_finish(f, h, m):
        wait_bytes(rx.at[f, h, m], axr.at[f, h, m])

    def send_out(a, h, cc, own_chip):
        def remote(p):
            pltpu.make_async_remote_copy(
                src_ref=stage.at[a, h, rows_of(p)],
                dst_ref=outs[a].at[:, cols(line[h], h)],
                send_sem=out_send.at[a, h],
                recv_sem=out_recv.at[a, h],
                device_id=ldev(h, p),
                device_id_type=MESH,
            ).start()

        @pl.when(jnp.logical_not(own_chip))
        def _():
            for core in range(NC):
                remote(cc * NC + core)

        @pl.when(own_chip)
        def _():
            remote(chip[h] * NC + (1 - c))
            pltpu.make_async_copy(
                stage.at[a, h, rows_of(line[h])], outs[a].at[:, cols(line[h], h)], out_loc.at[a, h]
            ).start()

    def chunk_of(h, j):
        cc = lax.rem(chip[h] + 2 + j + j // 2 + 2 * (j // 3), NY)
        return cc, pl.ds(pl.multiple_of(cc * CHUNK, CHUNK), CHUNK)

    def query_side(h):
        qr = buf[2, h]
        orr = buf[3, h]
        ng = full[0, h, 0:DH]
        nu = full[0, h, DH:2 * DH]
        gp = mm(qr, ng)
        up = mm(qr, nu)
        qd = mm_rt(orr, full[0, h, 2 * DH:3 * DH])
        s, act, rest, slope = silu_parts(gp)
        hd = (act * up).astype(BF16)
        dg = (qd * up * slope).astype(BF16)
        du = (qd * act).astype(BF16)
        acc[1, h, 0:DH] = mm_lt(qr, dg)
        acc[1, h, DH:2 * DH] = mm_lt(qr, du)
        acc[1, h, 2 * DH:3 * DH] = mm_lt(hd, orr)
        stage[0, h] = (mm_rt(dg, ng) + mm_rt(du, nu)).astype(BF16)

    def back(h, j):
        yy, rows = chunk_of(h, j)
        kr = buf[0, h, rows]
        ag = full[1, h, 0:DH]
        au = full[1, h, DH:2 * DH]
        ad = full[1, h, 2 * DH:3 * DH]
        bdg = mm(kr, ag)
        bdu = mm(kr, au)
        bh = mm_rt(scaled[h, rows], ad)
        gp = gate[h, rows]
        up = upper[h, rows]
        kd = dhid[h, rows]
        s, act, rest, slope = silu_parts(gp)
        twice = s + s
        curve = rest * (twice + act * (1.0 - twice))
        bdh = (bdg * up * slope + bdu * act).astype(BF16)
        bg = (bdg * kd * up * curve + (bdu * kd + bh * up) * slope).astype(BF16)
        bu = (bdg * kd * slope + bh * act).astype(BF16)
        kg = mm_rt(dgate[h, rows], ag) + mm_rt(dup[h, rows], au)
        kg = kg + mm_rt(bg, w[h, 0:DH]) + mm_rt(bu, w[h, DH:2 * DH])
        stage[1, h, rows] = kg.astype(BF16)
        vg = mm(hid[h, rows], ad) + mm(bdh, w[h, 2 * DH:3 * DH])
        stage[2, h, rows] = (rates(h, rows) * vg).astype(BF16)
        return yy

    def key_back():
        def step(j, carry):
            spots_of = (back(0, j), back(1, j))
            for a in (1, 2):
                for h in range(2):
                    send_out(a, h, spots_of[h], j == NY - 1)
            return carry

        lax.fori_loop(0, NY, step, 0)

    def send_query(h):
        for j in range(NY):
            cc, rows = chunk_of(h, j)
            if j < NY - 1:
                send_out(0, h, cc, False)
            else:
                send_out(0, h, cc, True)

    weights_first()
    for which in ((6,), (0, 1, 2, 3), (4, 5)):
        for a in (0, 1):
            for h in (0, 1):
                send_in(a, h, which)
    weights_second()
    for cp in wcp:
        cp.wait()
    for off in (0, 1, 3):
        key_forward(0, off)
    weights_third()
    for off in (0, 1, 3):
        key_forward(1, off)
    key_forward(0, 2)
    for m in range(3):
        rs_x_start(0, 0, m)
    key_forward(1, 2)
    for m in range(3):
        rs_x_start(0, 1, m)
    send_in(2, 1)
    send_in(3, 1)
    send_in(2, 0)
    send_in(3, 0)
    for step in (rs_x_finish, rs_z_finish, ag_z_finish):
        for h in range(2):
            for m in range(3):
                step(0, h, m)
    for h in range(2):
        for m in range(3):
            ag_x_finish(0, h, m)
        for off in range(NY):
            wait_in(2, h, off)
            wait_in(3, h, off)
        query_side(h)
        for m in range(3):
            rs_x_start(1, h, m)
    for h in range(2):
        send_query(h)
    for step in (rs_x_finish, rs_z_finish, ag_z_finish, ag_x_finish):
        for h in range(2):
            for m in range(3):
                step(1, h, m)
    key_back()

    @pl.when(diagonal)
    def _():
        wait_bytes(wz.at[pl.ds(0, 3)], w1s)

    wait_bytes(wz.at[pl.ds(0, NZ - 1)], w2s)
    wait_bytes(lq.at[pl.ds(0, 3)], l1s)
    wait_bytes(lq.at[pl.ds(0, 3)], l2s)
    for h in range(2):
        for a in range(4):
            wait_bytes(buf.at[a, h, pl.ds(0, ALL - ROWS)], in_send.at[a, h])
        for f in range(2):
            for m in range(3):
                wait_bytes(rx.at[f, h, m], xs.at[f, h, m])
                wait_bytes(rz.at[f, h, m], zsd.at[f, h, m])
                wait_bytes(rz.at[f, h, m], azs.at[f, h, m])
                wait_bytes(rx.at[f, h, m], axs.at[f, h, m])
        for a in range(3):
            wait_bytes(stage.at[a, h, pl.ds(0, ALL - ROWS)], out_send.at[a, h])
            wait_bytes(stage.at[a, h, pl.ds(0, ALL - ROWS)], out_recv.at[a, h])
            wait_bytes(stage.at[a, h, pl.ds(0, ROWS)], out_loc.at[a, h])


def body(queries, key_tokens, values, out_grad, learn_rates, w_gate, w_up, w_down):
    scale = 1.0 / math.sqrt(DH * ALL * NX * NZ)
    dma = pltpu.SemaphoreType.DMA
    out = jax.ShapeDtypeStruct(queries.shape, BF16)
    return pl.pallas_call(
        functools.partial(kernel, scale),
        out_shape=(out, out, out),
        in_specs=[pl.BlockSpec(memory_space=pl.ANY)] * 8,
        out_specs=[pl.BlockSpec(memory_space=pl.ANY)] * 3,
        scratch_shapes=[
            pltpu.VMEM((4, 2, ALL, DH), BF16),
            pltpu.VMEM((2, ALL, 128), F32),
            pltpu.VMEM((2, ALL), F32),
            pltpu.VMEM((NY, 8, CHUNK), F32),
            pltpu.VMEM((NY, 8, CHUNK), F32),
            pltpu.VMEM((NX, 8, CHUNK), F32),
            pltpu.VMEM((NZ, 3, EIGHTH, DH), BF16),
            pltpu.VMEM((2, 3 * DH, DH), BF16),
            pltpu.VMEM((2, 2, 3 * DH, DH), F32),
            pltpu.VMEM((2, 2, 3 * DH, DH), BF16),
            pltpu.VMEM((2, 2, 3, NX - 1, PART, DH), BF16),
            pltpu.VMEM((2, 2, 3, PART, DH), F32),
            pltpu.VMEM((2, 2, 3, PART, DH), BF16),
            pltpu.VMEM((2, 2, 3, NZ - 1, ZROWS, ZCOLS), BF16),
            pltpu.VMEM((2, 2, 3 * DH, DH), BF16),
            pltpu.VMEM((2, ALL, DH), F32),
            pltpu.VMEM((2, ALL, DH), F32),
            pltpu.VMEM((2, ALL, DH), F32),
            pltpu.VMEM((2, ALL, DH), BF16),
            pltpu.VMEM((2, ALL, DH), BF16),
            pltpu.VMEM((2, ALL, DH), BF16),
            pltpu.VMEM((2, ALL, DH), BF16),
            pltpu.VMEM((3, 2, ALL, DH), BF16),
            dma((4, 2)), dma((4, 2, NY)), dma((4, 2)), dma((2, 3)), dma,
            dma, dma, dma, dma, dma, dma, dma, dma,
            dma((2, 2, 3)), dma((2, 2, 3)), dma((2, 2, 3)), dma((2, 2, 3)),
            dma((2, 2, 3)), dma((2, 2, 3)), dma((2, 2, 3)), dma((2, 2, 3)),
            dma((3, 2)), dma((3, 2)), dma((3, 2)),
        ],
        compiler_params=pltpu.CompilerParams(
            collective_id=0, has_side_effects=True, vmem_limit_bytes=60 << 20
        ),
    )(queries, key_tokens, values, out_grad, learn_rates.T, w_gate, w_up, w_down)


def solution(mesh):
    tokens = P(("tok", "head"), None)
    heads = P("head", None, None)
    return jax.shard_map(
        body,
        mesh=mesh,
        in_specs=(tokens, tokens, tokens, tokens, P("tok", "head"), heads, heads, heads),
        out_specs=(tokens, tokens, tokens),
        check_vma=False,
    )
```
